32 devices in a mesh: tm: 2 (over x), tensor: 4 (over y, core), dp: 4 (over z).
Axes of the slice: x: 2, y: 2, z: 4, core: 2. Of those that a mesh axis runs over, the one named last changes fastest.
Arguments:
- video: bfloat16 [4, 2, 256, 1280], P('dp', 'tm'), may hold values from -6 to 6
- w_spatial: bfloat16 [3, 1280, 1280], P(None, 'dp', 'tensor'), as said below
- w_spatial_out: bfloat16 [1280, 1280], P('tensor', 'dp'), may hold values from -0.15625 to 0.15625
- temporal_weight: bfloat16 [3, 1280, 1280], P(None, 'dp', 'tensor'), as said below
- temporal_output_weight: bfloat16 [1280, 1280], P('tensor', 'dp'), may hold values from -0.15625 to 0.15625
- merger: bfloat16 [4, 1280, 8192], P(None, 'tensor', 'tm'), may hold values from -0.078125 to 0.078125
- text: bfloat16 [512, 8192], P('dp', 'tm'), may hold values from -6 to 6
- norm_gain: float32 [8192], P('tm'), may hold values from 0.1 to 1.9
- w_gate: bfloat16 [8192, 15360], P('tm', ('tensor', 'dp')), may hold values from -0.0625 to 0.0625
- w_up: bfloat16 [8192, 15360], P('tm', ('tensor', 'dp')), may hold values from -0.0625 to 0.0625
- w_down: bfloat16 [15360, 8192], P(('tensor', 'dp'), 'tm'), may hold values from -0.046875 to 0.046875
- probe: bfloat16 [512, 8192], P(None, 'tm'), may hold values from -0.25 to 0.25
- ref_margin: float32 [16], replicated, may hold values from -0.5 to 0.5
- pair_ids: int32 [512], replicated, may hold values from 0 to 3
- labels: int32 [512], replicated, may hold values from -1 to 1
- positions: int32 [512], P('dp'), may hold values from 0 to 127
Outputs:
- losses: float32 [16], replicated
- grad_gate: bfloat16 [8192, 15360], P('tm', ('tensor', 'dp'))
- grad_up: bfloat16 [8192, 15360], P('tm', ('tensor', 'dp'))
- grad_down: bfloat16 [15360, 8192], P(('tensor', 'dp'), 'tm')
The draws below stay inside these ranges and needn't reach their ends.
Inputs may be any that keep to these rules, and one draw needn't show every extreme that they name: `w_spatial`: queries, keys and values in this order along the first dimension. `temporal_weight`: queries, keys and values in this order along the first dimension. `labels`: 1 for a chosen rollout's row, -1 for a rejected one's, 0 for a row outside the loss. `positions`: index f * 64 + g of the merged token, frame f and group g of four consecutive patches.
All inputs are finite; a program needn't handle non-finite values.
Results may differ from the reference program's by a relative error of at most 0.035.
Values may be sent and summed in bfloat16 or wider, within the bound.
A program may use at most 128 MiB of HBM per device.

```python
import math
import jax
import jax.numpy as jnp
from jax import lax

W = 1280
HEADS = 16
P_SIZE = 256
F = 2
D = 8192
FF = 15360
ROWS = 128
R_ALL = 512
PAIRS_DEV = 4
PAIRS = 16
N_DP = 4


def drawn_projections(base_key):
    normal_draw = jax.random.normal(jax.random.fold_in(base_key, 11), (3, W, W), jnp.float32)
    return normal_draw / math.sqrt(W)


def draw_w_spatial(key, part):
    return drawn_projections(jax.random.fold_in(key, 101)).astype(jnp.bfloat16)


def draw_temporal_weight(key, part):
    return drawn_projections(jax.random.fold_in(key, 202)).astype(jnp.bfloat16)


def set_ends(values, rng, smallest, high):
    longest = values.shape.index(max(values.shape))
    spots = []
    for shift in (0, 1):
        where = [jax.random.randint(jax.random.fold_in(rng, axis), (), 0, length) for axis, length in enumerate(values.shape)]
        where[longest] = (where[longest] + shift) % values.shape[longest]
        spots.append(tuple(where))
    return values.at[spots[0]].set(smallest).at[spots[1]].set(high)


def shard_levels(own_key, shape, shards, least, high):
    loudness = 1.0
    for axis_at, shards_of in shards:
        steps = jax.random.uniform(jax.random.fold_in(jax.random.fold_in(own_key, 6), axis_at), (shards_of,), jnp.float32, least / len(shards), high / len(shards))
        loudness = loudness * jnp.repeat(jnp.exp(steps), shape[axis_at] // shards_of).reshape((-1,) + (1,) * (len(shape) - 1 - axis_at))
    return loudness


def scatter_about(key, extent, deviation, reach, shards=(), kind=jnp.bfloat16):
    factor_of = shard_levels(key, extent, shards, -0.22, 0.18) if shards else 1.0
    values = jax.random.normal(key, extent, jnp.float32) * deviation * factor_of
    return jnp.minimum(jnp.maximum(values, -reach), reach).astype(kind)


def setup_inputs(seed: int = 0) -> dict:
    streams_of = jax.random.split(jax.random.key(seed), 17)
    video = scatter_about(streams_of[0], (N_DP, F, P_SIZE, W), 1.0, 6.0, ((0, 4), (1, 2)))
    w_spatial = draw_w_spatial(jax.random.fold_in(streams_of[16], 71), 0)
    w_spatial_out = scatter_about(streams_of[2], (W, W), W ** -0.5, 0.15625, ((0, 4), (1, 4)))
    temporal_weight = draw_temporal_weight(jax.random.fold_in(streams_of[16], 71), 0)
    temporal_output_weight = scatter_about(streams_of[4], (W, W), W ** -0.5, 0.15625, ((0, 4), (1, 4)))
    merger = scatter_about(streams_of[5], (4, W, D), (4 * W) ** -0.5, 0.078125, ((1, 4), (2, 2)))
    text = scatter_about(streams_of[6], (R_ALL, D), 1.0, 6.0, ((0, 4), (1, 2)))
    norm_gain = jnp.clip(1.0 + 0.18 * jax.random.normal(streams_of[7], (D,), jnp.float32), 0.1, 1.9)
    w_gate = scatter_about(streams_of[8], (D, FF), D ** -0.5, 0.0625, ((0, 2), (1, 16)))
    w_up = scatter_about(streams_of[9], (D, FF), D ** -0.5, 0.0625, ((0, 2), (1, 16)))
    w_down = scatter_about(streams_of[10], (FF, D), FF ** -0.5, 0.046875, ((0, 16), (1, 2)))
    probe = scatter_about(streams_of[11], (R_ALL, D), (D // 16) ** -0.5, 0.25, ((1, 2),))
    ref_margin = jnp.clip(jax.random.uniform(streams_of[12], (PAIRS,), jnp.float32, -0.5, 0.5), -0.5, 0.5)
    pair_ids = set_ends(jax.random.randint(streams_of[13], (R_ALL,), 0, PAIRS_DEV), jax.random.fold_in(streams_of[13], 1), 0, PAIRS_DEV - 1).astype(jnp.int32)
    labels = set_ends(jax.random.randint(streams_of[14], (R_ALL,), -1, 2), jax.random.fold_in(streams_of[14], 1), -1, 1).astype(jnp.int32)
    positions = set_ends(jax.random.randint(streams_of[15], (R_ALL,), 0, F * P_SIZE // 4), jax.random.fold_in(streams_of[15], 1), 0, (F * P_SIZE // 4) - 1).astype(jnp.int32)
    return dict(video=video, w_spatial=w_spatial, w_spatial_out=w_spatial_out, temporal_weight=temporal_weight, temporal_output_weight=temporal_output_weight, merger=merger, text=text, norm_gain=norm_gain, w_gate=w_gate, w_up=w_up, w_down=w_down, probe=probe, ref_margin=ref_margin, pair_ids=pair_ids, labels=labels, positions=positions)


beta_scale = 0.1
loss_scale = 256.0
norm_eps = 1e-06

def layer_norm(values):
    centered = values - lax.optimization_barrier(jnp.mean(values, axis=-1, keepdims=True))
    spread = lax.optimization_barrier(jnp.mean(centered * centered, axis=-1, keepdims=True))
    return centered * lax.rsqrt(spread + norm_eps)

def attend(queries, key_rows, value_rows, head_size):
    leading = queries.shape[:-1]
    head_count = queries.shape[-1] // head_size

    def head_split(tensor_in):
        return tensor_in.astype(jnp.float32).reshape(tensor_in.shape[:-1] + (head_count, head_size))
    scores = jnp.einsum('...qhd,...khd->...hqk', head_split(queries), head_split(key_rows)) * head_size ** (-0.5)
    weights_soft = jax.nn.softmax(scores, axis=-1).astype(jnp.bfloat16)
    attended_context = jnp.einsum('...hqk,...khd->...qhd', weights_soft.astype(jnp.float32), head_split(value_rows))
    return attended_context.astype(jnp.bfloat16).reshape(leading + (head_count * head_size,))

def reference(video, w_spatial, w_spatial_out, temporal_weight, temporal_output_weight, merger, text, norm_gain, w_gate, w_up, w_down, probe, ref_margin, pair_ids, labels, positions):
    head_size = W // HEADS

    def spatial_frame(one_frame):
        normed_input = layer_norm(one_frame.astype(jnp.float32)).astype(jnp.bfloat16)
        query_slice = jnp.dot(normed_input, w_spatial[0], preferred_element_type=jnp.float32).astype(jnp.bfloat16)
        key_slice = jnp.dot(normed_input, w_spatial[1], preferred_element_type=jnp.float32).astype(jnp.bfloat16)
        value_slice = jnp.dot(normed_input, w_spatial[2], preferred_element_type=jnp.float32).astype(jnp.bfloat16)
        attended_context = attend(query_slice, key_slice, value_slice, head_size)
        return (one_frame.astype(jnp.float32) + jnp.dot(attended_context, w_spatial_out, preferred_element_type=jnp.float32)).astype(jnp.bfloat16)
    mixed = lax.map(spatial_frame, video.reshape(N_DP * F, P_SIZE, W)).reshape(N_DP, F, P_SIZE, W)

    def temporal_video(one_clip):
        normed_input = layer_norm(one_clip.astype(jnp.float32)).astype(jnp.bfloat16).astype(jnp.float32)
        query_slice = jnp.einsum('oly,yt->lot', normed_input, temporal_weight[0].astype(jnp.float32)).astype(jnp.bfloat16)
        key_slice = jnp.einsum('oly,yt->lot', normed_input, temporal_weight[1].astype(jnp.float32)).astype(jnp.bfloat16)
        value_slice = jnp.einsum('oly,yt->lot', normed_input, temporal_weight[2].astype(jnp.float32)).astype(jnp.bfloat16)
        attended_context = attend(query_slice, key_slice, value_slice, head_size)
        residual_update = jnp.einsum('lby,yd->bld', attended_context.astype(jnp.float32), temporal_output_weight.astype(jnp.float32))
        return (one_clip.astype(jnp.float32) + residual_update).astype(jnp.bfloat16)
    encoded = lax.map(temporal_video, mixed)
    per_video = F * (P_SIZE // 4)
    flat_tokens = encoded.reshape(N_DP * per_video, 4 * W)
    video_index = jnp.arange(R_ALL, dtype=jnp.int32) // ROWS
    picked = flat_tokens[(video_index * per_video + positions).astype(jnp.int32)]
    visual = jnp.dot(picked, merger.reshape(4 * W, D), preferred_element_type=jnp.float32)
    hidden_in = text.astype(jnp.float32) + visual
    mean_square = lax.optimization_barrier(jnp.mean(hidden_in * hidden_in, axis=1, keepdims=True))
    normed_rows = (hidden_in * lax.rsqrt(mean_square + norm_eps) * norm_gain[None, :]).astype(jnp.bfloat16)
    gate_pre = jnp.dot(normed_rows, w_gate, preferred_element_type=jnp.float32)
    up_pre = jnp.dot(normed_rows, w_up, preferred_element_type=jnp.float32)
    sig_gate = jax.nn.sigmoid(gate_pre)
    hidden = (gate_pre * sig_gate * up_pre).astype(jnp.bfloat16)
    delta = jnp.dot(hidden, w_down, preferred_element_type=jnp.float32)
    probe_wide = probe.astype(jnp.float32)
    score = lax.optimization_barrier(jnp.sum(delta * probe_wide, axis=1))
    global_pair = video_index * PAIRS_DEV + pair_ids
    member = (global_pair[:, None] == jnp.arange(PAIRS, dtype=jnp.int32)[None, :]).astype(jnp.float32)
    signed = labels.astype(jnp.float32)
    margin = jnp.dot(signed * score, member, precision=lax.Precision.HIGHEST)
    logits = beta_scale * margin - ref_margin
    losses = jax.nn.softplus(-logits)
    coefficient = -beta_scale * loss_scale * jax.nn.sigmoid(-logits)
    row_coef = jnp.dot(member, coefficient, precision=lax.Precision.HIGHEST) * signed
    cotangent = (row_coef[:, None] * probe_wide).astype(jnp.bfloat16)
    grad_down = jnp.dot(hidden.T, cotangent, preferred_element_type=jnp.float32).astype(jnp.bfloat16)
    hidden_grad = jnp.dot(cotangent, w_down.T, preferred_element_type=jnp.float32)
    gate_grad = (hidden_grad * up_pre * sig_gate * (1.0 + gate_pre * (1.0 - sig_gate))).astype(jnp.bfloat16)
    up_grad = (hidden_grad * gate_pre * sig_gate).astype(jnp.bfloat16)
    grad_gate = jnp.dot(normed_rows.T, gate_grad, preferred_element_type=jnp.float32).astype(jnp.bfloat16)
    grad_up = jnp.dot(normed_rows.T, up_grad, preferred_element_type=jnp.float32).astype(jnp.bfloat16)
    return (losses, grad_gate, grad_up, grad_down)
```

```python
import jax
import jax.numpy as jnp
from jax import lax
from jax.sharding import PartitionSpec as P

W = 1280
HEADS = 16
D = 8192
ROWS = 128
PAIRS_DEV = 4


beta_scale = 0.1
loss_scale = 256.0
norm_eps = 1e-06


def layer_norm(values):
    centered = values - jnp.mean(values, axis=-1, keepdims=True)
    spread = jnp.mean(centered * centered, axis=-1, keepdims=True)
    return centered * lax.rsqrt(spread + norm_eps)


def attend(queries, key_rows, value_rows, head_size):
    leading = queries.shape[:-1]
    head_count = queries.shape[-1] // head_size

    def head_split(tensor_in):
        return tensor_in.reshape(tensor_in.shape[:-1] + (head_count, head_size))

    scores = jnp.einsum(
        "...qhd,...khd->...hqk",
        head_split(queries),
        head_split(key_rows),
        preferred_element_type=jnp.float32,
    ) * head_size ** (-0.5)
    weights_soft = jax.nn.softmax(scores, axis=-1).astype(jnp.bfloat16)
    attended_context = jnp.einsum(
        "...hqk,...khd->...qhd",
        weights_soft,
        head_split(value_rows),
        preferred_element_type=jnp.float32,
    )
    return attended_context.astype(jnp.bfloat16).reshape(leading + (head_count * head_size,))


def body(
    video,
    w_spatial,
    w_spatial_out,
    temporal_weight,
    temporal_output_weight,
    merger,
    text,
    norm_gain,
    w_gate,
    w_up,
    w_down,
    probe,
    ref_margin,
    pair_ids,
    labels,
    positions,
):
    head_size = W // HEADS
    tensor_count = lax.axis_size("tensor")
    tensor_index = lax.axis_index("tensor")
    tm_index = lax.axis_index("tm")
    total_rows = probe.shape[0]
    probe_part = lax.dot_general(
        probe, w_down, (((1,), (1,)), ((), ())), preferred_element_type=jnp.float32
    ).astype(jnp.bfloat16)

    def gathered(qkv, out):
        whole = lax.all_gather(jnp.concatenate([qkv, out[None]], axis=0), "dp", axis=0)
        n, _, rows, cols = whole.shape
        return (
            whole[:, :3].transpose(1, 0, 2, 3).reshape(3, n * rows, cols),
            whole[:, 3].transpose(1, 0, 2).reshape(rows, n * cols),
        )

    spatial_w, spatial_out = gathered(w_spatial, w_spatial_out)
    temporal_weight, temporal_output_weight, spatial_w, probe_part = lax.optimization_barrier(
        (temporal_weight, temporal_output_weight, spatial_w, probe_part)
    )
    temporal_w, temporal_output = gathered(temporal_weight, temporal_output_weight)
    probe_down = lax.psum_scatter(probe_part, "tm", scatter_dimension=0, tiled=True)
    temporal_w, probe_down = lax.optimization_barrier((temporal_w, probe_down))
    frames = video[0]
    patches = frames.shape[1]
    width = frames.shape[2]

    def spatial_frame(one_frame):
        normed_input = layer_norm(one_frame.astype(jnp.float32)).astype(jnp.bfloat16)
        project = jnp.einsum(
            "pw,jwc->jpc", normed_input, spatial_w, preferred_element_type=jnp.float32
        ).astype(jnp.bfloat16)
        attended_context = attend(project[0], project[1], project[2], head_size)
        return jnp.dot(attended_context, spatial_out, preferred_element_type=jnp.float32)

    partial_out = lax.map(spatial_frame, frames)
    summed = lax.psum(partial_out.astype(jnp.bfloat16), "tensor").astype(jnp.float32)
    mixed = (frames.astype(jnp.float32) + summed).astype(jnp.bfloat16)
    arrived = lax.all_to_all(mixed, "tm", split_axis=1, concat_axis=0, tiled=True)
    frame_count = arrived.shape[0]
    normed_t = layer_norm(arrived.astype(jnp.float32)).astype(jnp.bfloat16)
    project_t = jnp.einsum(
        "fpw,jwc->jpfc", normed_t, temporal_w, preferred_element_type=jnp.float32
    ).astype(jnp.bfloat16)
    temporal_context = attend(project_t[0], project_t[1], project_t[2], head_size)
    partial_t = jnp.einsum(
        "lby,yd->bld", temporal_context, temporal_output, preferred_element_type=jnp.float32
    )
    temporal_sum = lax.psum_scatter(
        partial_t.astype(jnp.bfloat16), "tensor", scatter_dimension=2, tiled=True
    ).astype(jnp.float32)
    quarter = width // tensor_count
    residual_cols = lax.dynamic_slice_in_dim(arrived, tensor_index * quarter, quarter, 2)
    encoded = (residual_cols.astype(jnp.float32) + temporal_sum).astype(jnp.bfloat16)
    groups_local = encoded.shape[1] // 4
    merged = encoded.reshape(frame_count * groups_local, 4 * quarter)
    groups_frame = patches // 4
    frame_of = positions // groups_frame
    group_of = positions % groups_frame
    owner_tm = group_of // groups_local
    slot_group = group_of % groups_local
    slot_index = frame_of * groups_local + slot_group
    hit_table = (
        slot_index[:, None] == jnp.arange(frame_count * groups_local, dtype=jnp.int32)[None, :]
    ) & (owner_tm == tm_index)[:, None]
    picked = jnp.dot(hit_table.astype(jnp.bfloat16), merged, preferred_element_type=jnp.float32)
    chosen_tokens = lax.psum(picked.astype(jnp.bfloat16), "tm")
    vis_part = jnp.dot(
        chosen_tokens,
        merger.reshape(4 * quarter, merger.shape[2]),
        preferred_element_type=jnp.float32,
    )
    visual = lax.psum_scatter(
        vis_part.astype(jnp.bfloat16), "tensor", scatter_dimension=0, tiled=True
    ).astype(jnp.float32)
    own_rows = visual.shape[0]
    text_own = lax.dynamic_slice_in_dim(text, tensor_index * own_rows, own_rows, 0)
    hidden_in = text_own.astype(jnp.float32) + visual
    square_sum = lax.psum(jnp.sum(hidden_in * hidden_in, axis=1), "tm")
    normed_rows = (
        hidden_in * lax.rsqrt(square_sum / D + norm_eps)[:, None] * norm_gain[None, :]
    ).astype(jnp.bfloat16)
    all_rows = lax.all_gather(normed_rows, ("dp", "tensor"), axis=0, tiled=True)
    hidden_cols = w_gate.shape[1]
    row_block = all_rows
    gate_up = lax.psum_scatter(
        jnp.concatenate(
            [
                jnp.dot(row_block, w_gate, preferred_element_type=jnp.float32),
                jnp.dot(row_block, w_up, preferred_element_type=jnp.float32),
            ],
            axis=1,
        ).astype(jnp.bfloat16),
        "tm",
        scatter_dimension=0,
        tiled=True,
    ).astype(jnp.float32)
    gate_pre = gate_up[:, :hidden_cols]
    up_pre = gate_up[:, hidden_cols:]
    sig_gate = jax.nn.sigmoid(gate_pre)
    hidden_local = (gate_pre * sig_gate * up_pre).astype(jnp.bfloat16)
    probe_grad = probe_down.astype(jnp.float32)
    gate_slope = (probe_grad * up_pre * sig_gate * (1.0 + gate_pre * (1.0 - sig_gate))).astype(
        jnp.bfloat16
    )
    up_slope = (probe_grad * gate_pre * sig_gate).astype(jnp.bfloat16)
    pair_total = ref_margin.shape[0]
    row_index = jnp.arange(total_rows, dtype=jnp.int32)
    global_pair = row_index // ROWS * PAIRS_DEV + pair_ids
    member = (global_pair[:, None] == jnp.arange(pair_total, dtype=jnp.int32)[None, :]).astype(
        jnp.float32
    )
    signed = labels.astype(jnp.float32)
    local_rows = hidden_local.shape[0]
    score = jnp.sum(hidden_local.astype(jnp.float32) * probe_grad, axis=1)
    margin = jnp.dot(
        lax.dynamic_slice_in_dim(signed, tm_index * local_rows, local_rows, 0) * score,
        lax.dynamic_slice_in_dim(member, tm_index * local_rows, local_rows, 0),
        precision=lax.Precision.HIGHEST,
    )
    for axis in ("tensor", "dp", "tm"):
        margin = lax.optimization_barrier(lax.psum(margin, axis))
    shared = lax.all_gather(
        jnp.concatenate([hidden_local, gate_slope, up_slope], axis=1), "tm", axis=0, tiled=True
    )
    hidden_all = shared[:, :hidden_cols]
    logits = beta_scale * margin - ref_margin
    losses = jax.nn.softplus(-logits)
    coefficient = -beta_scale * loss_scale * jax.nn.sigmoid(-logits)
    row_coef = jnp.dot(member, coefficient, precision=lax.Precision.HIGHEST) * signed
    cotangent = (row_coef[:, None] * probe.astype(jnp.float32)).astype(jnp.bfloat16)
    grads = (row_coef[:, None] * shared[:, hidden_cols:].astype(jnp.float32)).astype(jnp.bfloat16)

    def over_rows(left, right):
        return lax.dot_general(
            left, right, (((0,), (0,)), ((), ())), preferred_element_type=jnp.float32
        ).astype(jnp.bfloat16)

    return (
        losses,
        over_rows(all_rows, grads[:, :hidden_cols]),
        over_rows(all_rows, grads[:, hidden_cols:]),
        over_rows(hidden_all, cotangent),
    )


def solution(mesh):
    return jax.shard_map(
        body,
        mesh=mesh,
        in_specs=(
            P("dp", "tm", None, None),
            P(None, "dp", "tensor"),
            P("tensor", "dp"),
            P(None, "dp", "tensor"),
            P("tensor", "dp"),
            P(None, "tensor", "tm"),
            P("dp", "tm"),
            P("tm"),
            P("tm", ("tensor", "dp")),
            P("tm", ("tensor", "dp")),
            P(("tensor", "dp"), "tm"),
            P(None, "tm"),
            P(),
            P(),
            P(),
            P("dp"),
        ),
        out_specs=(
            P(),
            P("tm", ("tensor", "dp")),
            P("tm", ("tensor", "dp")),
            P(("tensor", "dp"), "tm"),
        ),
        check_vma=False,
    )
```
